1024 devices in a mesh: dp: 32 (over y, x, core), ctx: 32 (over z).
Axes of the slice: x: 4, y: 4, z: 32, core: 2. Of those that a mesh axis runs over, the one named last changes fastest.
Arguments:
- queries: bfloat16 [131072, 2048], P(('dp', 'ctx')), may hold values from -120 to 120
- keys: bfloat16 [131072, 512], P(('dp', 'ctx')), may hold values from -5.5 to 5.5
- values: bfloat16 [131072, 512], P(('dp', 'ctx')), may hold values from -6 to 6
- output_gradient: bfloat16 [131072, 2048], P(('dp', 'ctx')), may hold values from -6 to 6
- doc_blocks: int32 [512], P('dp'), may hold values from 1 to 3, 1024 in all
- doc_pad: int32 [512], P('dp'), may hold values from 0 to 127
Outputs:
- attn_out: bfloat16 [131072, 2048], P(('dp', 'ctx'))
- grad_queries: bfloat16 [131072, 2048], P(('dp', 'ctx'))
- grad_keys: bfloat16 [131072, 512], P(('dp', 'ctx'))
- grad_values: bfloat16 [131072, 512], P(('dp', 'ctx'))
The draws below stay inside these ranges and needn't reach their ends.
All inputs are finite; a program needn't handle non-finite values. No bound on the sum of `doc_blocks` on one device may be relied on, other than what follows from the above.
Results may differ from the reference program's by a relative error of at most 0.02.
Values may be sent and summed in bfloat16 or wider, within the bound.
A program may use at most 32 MiB of HBM per device.

```python
import math
import jax
import jax.numpy as jnp
import numpy as np
from jax import lax

QUERY_HEADS = 16
KEY_VALUE_HEADS = 4
HEAD_SIZE = 128
DEVICE_TOKENS = 128
MOST_DOC_BLOCKS = 3
DOCS = 512
BLOCK_TOTAL = 1024
TOKEN_SLOTS = 131072


def draw_keys(key, part):
    reshaped_tensor = jnp.clip(jax.random.normal(jax.random.fold_in(key, 11), (TOKEN_SLOTS, KEY_VALUE_HEADS * HEAD_SIZE), jnp.float32), -5.0, 5.0)
    return reshaped_tensor.astype(jnp.bfloat16)


def draw_queries(key, part):
    base_queries = jnp.clip(jax.random.normal(jax.random.fold_in(key, 19), (TOKEN_SLOTS, QUERY_HEADS * HEAD_SIZE), jnp.float32), -5.0, 5.0)
    return base_queries.astype(jnp.bfloat16)


def with_ends(result, own_key, smallest, high):
    index_at = [jax.random.randint(jax.random.fold_in(own_key, axis), (), 0, length) for axis, length in enumerate(result.shape)]
    widest = result.shape.index(max(result.shape))
    beside = index_at[:widest] + [(index_at[widest] + 1) % result.shape[widest]] + index_at[widest + 1:]
    return result.at[tuple(index_at)].set(smallest).at[tuple(beside)].set(high)


def shard_levels(stream_key, dims, split, low, high):
    loudness, own = 1.0, jax.random.fold_in(stream_key, 6)
    for dim, shards_of in split:
        draws = jnp.exp(jax.random.uniform(jax.random.fold_in(own, dim), (shards_of,), jnp.float32, low / len(split), high / len(split)))
        loudness = loudness * jnp.repeat(draws, dims[dim] // shards_of).reshape([-1 if axis == dim else 1 for axis in range(len(dims))])
    return loudness


def split_up(number_of, total, most, slope):
    portions = [(1 << 20) // math.isqrt(grade ** slope) + 1 for grade in range(2, number_of + 1)]
    rest, holding = total - most - (number_of - 1), [1] * (number_of - 1)
    while rest > 0:
        candidates = [i for i in range(number_of - 1) if holding[i] < most]
        pool, left = sum([portions[i] for i in candidates]), rest
        for i in candidates:
            extra = min(most - holding[i], max(1, left * portions[i] // pool), rest)
            holding[i] = holding[i] + extra
            rest = rest - extra
    return np.array([most] + holding)


def uneven(rng, number_of, total, reach, skew):
    if number_of == 2:
        one = jax.random.randint(rng, (), max(1, total - reach), min(reach, total - 1) + 1)
        return jnp.stack([one, total - one])
    lengths = jnp.asarray(split_up(number_of, total, reach, skew), jnp.int32)
    twos = (number_of - 1) // 2
    giver, taker = lengths[1:1 + 2 * twos:2], lengths[2:2 + 2 * twos:2]
    margin = jnp.minimum(giver - 1, reach - taker)
    shifted = jax.random.randint(jax.random.fold_in(rng, 1), (twos,), 0, 1 << 20) % (margin + 1)
    lengths = lengths.at[1:1 + 2 * twos:2].set(giver - shifted).at[2:2 + 2 * twos:2].set(taker + shifted)
    return lengths[jax.random.permutation(jax.random.fold_in(rng, 2), number_of)]


def normal_values(stream_key, extent, spread, bound, pieces=(), kind=jnp.bfloat16):
    entries = spread * jax.random.normal(stream_key, extent, jnp.float32)
    if pieces:
        entries = entries * shard_levels(stream_key, extent, pieces, -0.22, 0.18)
    return jnp.clip(entries, -bound, bound).astype(kind)


def setup_inputs(seed: int = 0) -> dict:
    arg_keys = jax.random.split(jax.random.key(seed), 7)
    return {
        "queries": draw_queries(jax.random.fold_in(arg_keys[6], 71), 0),
        "keys": draw_keys(jax.random.fold_in(arg_keys[6], 71), 0),
        "values": normal_values(arg_keys[2], (TOKEN_SLOTS, KEY_VALUE_HEADS * HEAD_SIZE), 1.0, 6.0, ((0, 1024),)),
        "output_gradient": normal_values(arg_keys[3], (TOKEN_SLOTS, QUERY_HEADS * HEAD_SIZE), 1.0, 6.0, ((0, 1024),)),
        "doc_blocks": uneven(arg_keys[4], DOCS, BLOCK_TOTAL, MOST_DOC_BLOCKS, 1).astype(jnp.int32),
        "doc_pad": with_ends(jax.random.randint(arg_keys[5], (DOCS,), 0, DEVICE_TOKENS), jax.random.fold_in(arg_keys[5], 1), 0, DEVICE_TOKENS - 1).astype(jnp.int32),
    }


def rounded(tensor):
    return lax.optimization_barrier(tensor.astype(jnp.bfloat16)).astype(jnp.float32)

def block_meta(block_ids, starts, doc_sizes, doc_pads, token_rows, block_count):
    in_range = (block_ids >= 0) & (block_ids < block_count)
    doc_index = lax.optimization_barrier(jnp.sum((starts[None, :] <= block_ids[:, None]).astype(jnp.int32), axis=1)) - 1
    doc_index = jnp.where(in_range, doc_index, -1)
    one_hot = jnp.arange(starts.shape[0], dtype=jnp.int32)[None, :] == doc_index[:, None]
    doc_ends = lax.optimization_barrier(jnp.sum(jnp.where(one_hot, (starts + doc_sizes)[None, :] * token_rows - doc_pads[None, :], 0), axis=1))
    positions = block_ids[:, None] * token_rows + jnp.arange(token_rows, dtype=jnp.int32)[None, :]
    is_valid = (positions < doc_ends[:, None]) & in_range[:, None]
    doc_ids = jnp.broadcast_to(doc_index[:, None], positions.shape)
    return (doc_ids.reshape(-1), positions.reshape(-1), is_valid.reshape(-1))

def allowed_pairs(query_info, key_info):
    same_doc = query_info[0][:, None] == key_info[0][None, :]
    causal = key_info[1][None, :] <= query_info[1][:, None]
    return same_doc & causal & query_info[2][:, None] & key_info[2][None, :]

def scores_of(query_rows, key_rows, score_scale):
    return jnp.einsum('tkgd,skd->kgts', query_rows.astype(jnp.float32), key_rows.astype(jnp.float32)) * score_scale

def softmax_parts(score_f32, pair_mask, query_valid):
    masked = jnp.where(pair_mask, score_f32, -jnp.inf)
    row_peak = jnp.where(query_valid, lax.optimization_barrier(jnp.max(masked, axis=-1)), 0.0)
    row_total = lax.optimization_barrier(jnp.sum(jnp.where(pair_mask, jnp.exp(score_f32 - row_peak[..., None]), 0.0), axis=-1))
    log_total = row_peak + jnp.log(jnp.where(query_valid, row_total, 1.0))
    weight = jnp.where(pair_mask, jnp.exp(score_f32 - log_total[..., None]), 0.0)
    return (log_total, weight)

def reference(queries, keys, values, output_gradient, doc_blocks, doc_pad):
    head_group_width = QUERY_HEADS // KEY_VALUE_HEADS
    score_scale = HEAD_SIZE ** (-0.5)
    backward_distance = MOST_DOC_BLOCKS - 1
    starts = jnp.cumsum(doc_blocks) - doc_blocks
    blocked_queries = queries.reshape(BLOCK_TOTAL, DEVICE_TOKENS, KEY_VALUE_HEADS, head_group_width, HEAD_SIZE)
    gradient_blocks = output_gradient.reshape(BLOCK_TOTAL, DEVICE_TOKENS, KEY_VALUE_HEADS, head_group_width, HEAD_SIZE)
    blocked_keys = keys.reshape(BLOCK_TOTAL, DEVICE_TOKENS, KEY_VALUE_HEADS, HEAD_SIZE)
    blocked_values = values.reshape(BLOCK_TOTAL, DEVICE_TOKENS, KEY_VALUE_HEADS, HEAD_SIZE)
    empty_key_values = jnp.zeros((backward_distance, DEVICE_TOKENS, KEY_VALUE_HEADS, HEAD_SIZE), keys.dtype)
    padded_keys = jnp.concatenate([empty_key_values, blocked_keys], axis=0)
    padded_values = jnp.concatenate([empty_key_values, blocked_values], axis=0)
    single = jnp.zeros((1,), jnp.int32)
    span = jnp.arange(MOST_DOC_BLOCKS, dtype=jnp.int32)

    def meta(block_ids):
        return block_meta(block_ids, starts, doc_blocks, doc_pad, DEVICE_TOKENS, BLOCK_TOTAL)

    def near_of(current_block_index):
        neighbor_keys = lax.dynamic_slice_in_dim(padded_keys, current_block_index, MOST_DOC_BLOCKS, 0).reshape(MOST_DOC_BLOCKS * DEVICE_TOKENS, KEY_VALUE_HEADS, HEAD_SIZE)
        neighbor_values = lax.dynamic_slice_in_dim(padded_values, current_block_index, MOST_DOC_BLOCKS, 0).reshape(MOST_DOC_BLOCKS * DEVICE_TOKENS, KEY_VALUE_HEADS, HEAD_SIZE)
        query_info = meta(current_block_index + single)
        pair_mask = allowed_pairs(query_info, meta(current_block_index - backward_distance + span))
        return (neighbor_keys, neighbor_values, pair_mask, query_info[2])

    def forward_one(current_block_index):
        neighbor_keys, neighbor_values, pair_mask, query_valid = near_of(current_block_index)
        score_f32 = scores_of(blocked_queries[current_block_index], neighbor_keys, score_scale)
        log_total, weight = softmax_parts(score_f32, pair_mask, query_valid)
        attn = jnp.einsum('kgts,skd->tkgd', rounded(weight), neighbor_values.astype(jnp.float32))
        return (attn.astype(jnp.bfloat16), log_total)
    attention_result, lse_all = lax.map(forward_one, jnp.arange(BLOCK_TOTAL, dtype=jnp.int32))
    delta_all = jnp.einsum('ntkgd,ntkgd->nkgt', gradient_blocks.astype(jnp.float32), attention_result.astype(jnp.float32))

    def query_grad(current_block_index):
        neighbor_keys, neighbor_values, pair_mask, query_valid = near_of(current_block_index)
        score_f32 = scores_of(blocked_queries[current_block_index], neighbor_keys, score_scale)
        weight = jnp.where(pair_mask, jnp.exp(score_f32 - lse_all[current_block_index][..., None]), 0.0)
        dprob = jnp.einsum('tkgd,skd->kgts', gradient_blocks[current_block_index].astype(jnp.float32), neighbor_values.astype(jnp.float32))
        dscore = rounded(weight * (dprob - delta_all[current_block_index][..., None]))
        grad_q = jnp.einsum('kgts,skd->tkgd', dscore, neighbor_keys.astype(jnp.float32)) * score_scale
        return grad_q.astype(jnp.bfloat16)
    full_query_gradient = lax.map(query_grad, jnp.arange(BLOCK_TOTAL, dtype=jnp.int32))
    empty_queries = jnp.zeros((backward_distance, DEVICE_TOKENS, KEY_VALUE_HEADS, head_group_width, HEAD_SIZE), queries.dtype)
    padded_queries = jnp.concatenate([blocked_queries, empty_queries], axis=0)
    padded_gradients = jnp.concatenate([gradient_blocks, empty_queries], axis=0)
    empty_statistics = jnp.zeros((backward_distance, KEY_VALUE_HEADS, head_group_width, DEVICE_TOKENS), jnp.float32)
    padded_log_sum = jnp.concatenate([lse_all, empty_statistics], axis=0)
    padded_delta_rows = jnp.concatenate([delta_all, empty_statistics], axis=0)

    def key_grad(current_block_index):
        following_queries = lax.dynamic_slice_in_dim(padded_queries, current_block_index, MOST_DOC_BLOCKS, 0).reshape(MOST_DOC_BLOCKS * DEVICE_TOKENS, KEY_VALUE_HEADS, head_group_width, HEAD_SIZE)
        following_gradients = lax.dynamic_slice_in_dim(padded_gradients, current_block_index, MOST_DOC_BLOCKS, 0).reshape(MOST_DOC_BLOCKS * DEVICE_TOKENS, KEY_VALUE_HEADS, head_group_width, HEAD_SIZE)
        following_log_sum = lax.dynamic_slice_in_dim(padded_log_sum, current_block_index, MOST_DOC_BLOCKS, 0).transpose(1, 2, 0, 3).reshape(KEY_VALUE_HEADS, head_group_width, MOST_DOC_BLOCKS * DEVICE_TOKENS)
        following_delta = lax.dynamic_slice_in_dim(padded_delta_rows, current_block_index, MOST_DOC_BLOCKS, 0).transpose(1, 2, 0, 3).reshape(KEY_VALUE_HEADS, head_group_width, MOST_DOC_BLOCKS * DEVICE_TOKENS)
        pair_mask = allowed_pairs(meta(current_block_index + span), meta(current_block_index + single))
        score_f32 = scores_of(following_queries, blocked_keys[current_block_index], score_scale)
        weight = jnp.where(pair_mask, jnp.exp(score_f32 - following_log_sum[..., None]), 0.0)
        dprob = jnp.einsum('tkgd,skd->kgts', following_gradients.astype(jnp.float32), blocked_values[current_block_index].astype(jnp.float32))
        dscore = rounded(weight * (dprob - following_delta[..., None]))
        grad_k = jnp.einsum('kgts,tkgd->skd', dscore, following_queries.astype(jnp.float32)) * score_scale
        grad_v = jnp.einsum('kgts,tkgd->skd', rounded(weight), following_gradients.astype(jnp.float32))
        return (grad_k.astype(jnp.bfloat16), grad_v.astype(jnp.bfloat16))
    full_key_gradient, full_value_gradient = lax.map(key_grad, jnp.arange(BLOCK_TOTAL, dtype=jnp.int32))
    return (attention_result.reshape(TOKEN_SLOTS, QUERY_HEADS * HEAD_SIZE), full_query_gradient.reshape(TOKEN_SLOTS, QUERY_HEADS * HEAD_SIZE), full_key_gradient.reshape(TOKEN_SLOTS, KEY_VALUE_HEADS * HEAD_SIZE), full_value_gradient.reshape(TOKEN_SLOTS, KEY_VALUE_HEADS * HEAD_SIZE))
```

```python
import jax
import jax.numpy as jnp
from jax import lax
from jax.experimental import pallas as pl
from jax.experimental.pallas import tpu as pltpu
from jax.sharding import PartitionSpec as P

KV_HEADS = 4
GROUP = 4
D = 128
ROWS = 128
WIDE = GROUP * D
SCALE = D**-0.5
LOG2E = 1.4426950408889634
NEG = -1e30
X = 4
Y = 4
DP = 32
CTX = 32
MESH = pl.DeviceIdType.MESH


def dot(a, b, contract):
    return lax.dot_general(
        a, b, ((contract[:1], contract[1:]), ((), ())), preferred_element_type=jnp.float32
    )


def stacked(ref, h):
    return jnp.concatenate(
        [ref[:, h * WIDE + g * D : h * WIDE + (g + 1) * D] for g in range(GROUP)], axis=0
    )


def body(
    q_hbm, k_hbm, v_hbm, g_hbm, size_hbm, pad_hbm,
    o_hbm, dq_hbm, dk_hbm, dv_hbm,
    q, g, kv, size_row, pad_row, meta,
    t2, r2, u, ru, t1, t0, o, dq, dkv,
    in_sem, out_sem, f_send, f_recv, b_send, b_recv, m_send, m_recv,
):
    dp, ctx = lax.axis_index("dp"), lax.axis_index("ctx")
    block = dp * CTX + ctx
    after = lax.rem(block + 1, DP * CTX)
    ahead = (after // CTX, lax.rem(after, CTX))
    before = lax.rem(block + DP * CTX - 1, DP * CTX)
    behind = (before // CTX, lax.rem(before, CTX))
    core = lax.rem(dp, 2)
    x = lax.rem(dp // 2, X)
    y = dp // (2 * X)
    pair = (dp + 1 - 2 * core, ctx)
    along_x = [((y * X + lax.rem(x + j, X)) * 2 + core, ctx) for j in range(1, X)]
    along_y = [((lax.rem(y + j, Y) * X + x) * 2 + core, ctx) for j in range(1, Y)]

    tiny = [
        pltpu.make_async_copy(size_hbm, size_row, in_sem.at[0]),
        pltpu.make_async_copy(pad_hbm, pad_row, in_sem.at[1]),
    ]
    loads = []
    for h in range(KV_HEADS):
        cols = pl.ds(h * D, D)
        wide = pl.ds(h * WIDE, WIDE)
        loads.append([
            pltpu.make_async_copy(q_hbm.at[:, wide], q.at[:, wide], in_sem.at[2 + h * 4]),
            pltpu.make_async_copy(g_hbm.at[:, wide], g.at[:, wide], in_sem.at[3 + h * 4]),
            pltpu.make_async_copy(
                k_hbm.at[:, cols], kv.at[0, h, pl.ds(2 * ROWS, ROWS)], in_sem.at[4 + h * 4]),
            pltpu.make_async_copy(
                v_hbm.at[:, cols], kv.at[1, h, pl.ds(2 * ROWS, ROWS)], in_sem.at[5 + h * 4]),
        ])
    for c in tiny:
        c.start()

    barrier = pltpu.get_barrier_semaphore()
    peers = [ahead, behind, pair] + along_x + along_y
    for peer in peers:
        pl.semaphore_signal(barrier, inc=1, device_id=peer, device_id_type=MESH)
    for group in loads:
        for c in group:
            c.start()
    meta[pl.ds(dp, 1)] = jnp.zeros((1, 2, 128), jnp.int32)
    for c in tiny:
        c.wait()
    meta[pl.ds(dp, 1), 0:1, 0:16] = size_row[...].reshape(1, 1, 16)
    meta[pl.ds(dp, 1), 1:2, 0:16] = pad_row[...].reshape(1, 1, 16)
    pl.semaphore_wait(barrier, len(peers))

    def own_send(h):
        return [
            pltpu.make_async_remote_copy(
                src_ref=(k_hbm, v_hbm)[i].at[:, pl.ds(h * D, D)],
                dst_ref=kv.at[i, h, pl.ds(ROWS, ROWS)],
                send_sem=f_send.at[0, h, i], recv_sem=f_recv.at[0, h, i],
                device_id=ahead, device_id_type=MESH)
            for i in range(2)
        ]

    def relay_send(h):
        return [
            pltpu.make_async_remote_copy(
                src_ref=kv.at[i, h, pl.ds(ROWS, ROWS)],
                dst_ref=kv.at[i, h, pl.ds(0, ROWS)],
                send_sem=f_send.at[1, h, i], recv_sem=f_recv.at[1, h, i],
                device_id=ahead, device_id_type=MESH)
            for i in range(2)
        ]

    def back_send(stage, h, i):
        return pltpu.make_async_remote_copy(
            src_ref=(t2, u)[stage].at[i, h], dst_ref=(r2, ru)[stage].at[i, h],
            send_sem=b_send.at[stage, h, i], recv_sem=b_recv.at[stage, h, i],
            device_id=behind, device_id_type=MESH)

    def meta_send(first, count, device, slot):
        rows = meta.at[pl.ds(first, count)]
        return pltpu.make_async_remote_copy(
            src_ref=rows, dst_ref=rows, send_sem=m_send.at[slot], recv_sem=m_recv.at[slot],
            device_id=device, device_id_type=MESH)

    def landing(first, count, slot):
        rows = meta.at[pl.ds(first, count)]
        return pltpu.make_async_remote_copy(
            src_ref=rows, dst_ref=rows, send_sem=m_send.at[slot], recv_sem=m_recv.at[slot],
            device_id=pair, device_id_type=MESH)

    own = [own_send(h) for h in range(KV_HEADS)]
    relay = [relay_send(h) for h in range(KV_HEADS)]

    def start(copies):
        for c in copies:
            c.start()

    def relay_on(h):
        for a, b in zip(own[h], relay[h]):
            a.wait_recv()
            b.start()

    m1 = meta_send(dp, 1, pair, 0)
    m1.start()
    start(own[0])
    start(own[1])
    landing(dp + 1 - 2 * core, 1, 0).wait_recv()
    m2 = [meta_send(dp - core, 2, along_x[j - 1], j) for j in range(1, X)]
    start(m2)
    relay_on(0)
    start(own[2])
    for j in range(1, X):
        landing((y * X + lax.rem(x + X - j, X)) * 2, 2, j).wait_recv()
    m3 = [meta_send(y * X * 2, 2 * X, along_y[j - 1], X - 1 + j) for j in range(1, Y)]
    start(m3)
    relay_on(1)
    start(own[3])
    for j in range(1, Y):
        landing(lax.rem(y + Y - j, Y) * X * 2, 2 * X, X - 1 + j).wait_recv()

    sizes = meta[:, 0, :].astype(jnp.float32)
    pads = meta[:, 1, :].astype(jnp.float32)
    sizes16 = sizes.astype(jnp.bfloat16)
    below = (
        lax.broadcasted_iota(jnp.int32, (128, 128), 0)
        < lax.broadcasted_iota(jnp.int32, (128, 128), 1)
    )
    inside = dot(sizes16, jnp.where(below, 1.0, 0.0).astype(jnp.bfloat16), (1, 0))
    totals = dot(sizes16, jnp.ones((128, 128), jnp.bfloat16), (1, 0))
    over = (
        lax.broadcasted_iota(jnp.int32, (DP, DP), 1)
        < lax.broadcasted_iota(jnp.int32, (DP, DP), 0)
    )
    lead = dot(
        jnp.where(over, 1.0, 0.0).astype(jnp.bfloat16), totals.astype(jnp.bfloat16), (1, 0)
    )
    offset = block.astype(jnp.float32) - (inside + lead)
    mine = (offset >= 0.0) & (offset < sizes)

    def total(a):
        return jnp.sum(jnp.sum(a, axis=0, keepdims=True), axis=1, keepdims=True)

    place = total(jnp.where(mine, offset, 0.0))
    valid = total(
        jnp.where(mine, jnp.minimum((sizes - offset) * float(ROWS) - pads, float(ROWS)), 0.0)
    )
    bias2 = jnp.where(place >= 1.5, 0.0, NEG)
    bias1 = jnp.where(place >= 0.5, 0.0, NEG)
    slot = lax.broadcasted_iota(jnp.int32, (1, ROWS), 1).astype(jnp.float32)
    live1 = jnp.where(slot < valid, 1.0, 0.0)
    live = jnp.concatenate([live1] * GROUP, axis=1)
    tri1 = jnp.where(
        lax.broadcasted_iota(jnp.int32, (ROWS, ROWS), 0)
        <= lax.broadcasted_iota(jnp.int32, (ROWS, ROWS), 1),
        0.0, NEG,
    )
    tri = jnp.concatenate([tri1] * GROUP, axis=1)

    stores = []

    def store(src, dst, n):
        c = pltpu.make_async_copy(src, dst, out_sem.at[n])
        c.start()
        stores.append(c)

    back = {}

    def head(h):
        wide = pl.ds(h * WIDE, WIDE)
        for c in loads[h]:
            c.wait()
        qs, gs = stacked(q, h), stacked(g, h)
        for c in relay[h]:
            c.wait_recv()
        keys, vals = kv[0, h], kv[1, h]
        s = dot(keys, qs, (1, 1)) * (SCALE * LOG2E)
        s = jnp.concatenate(
            [s[:ROWS] + bias2, s[ROWS : 2 * ROWS] + bias1, s[2 * ROWS :] + tri], axis=0
        )
        e = jnp.exp2(s - jnp.max(s, axis=0, keepdims=True))
        p = e * (live / jnp.sum(e, axis=0, keepdims=True))
        p16 = p.astype(jnp.bfloat16)
        dval = dot(p16, gs, (1, 0))
        t2[1, h] = dval[:ROWS].astype(jnp.bfloat16)
        back[0, h, 1] = back_send(0, h, 1)
        back[0, h, 1].start()
        t1[1, h] = dval[ROWS : 2 * ROWS]
        t0[1, h] = dval[2 * ROWS :]
        dp_ = dot(vals, gs, (1, 1))
        delta = jnp.sum(p * dp_, axis=0, keepdims=True)
        ds = (p * (dp_ - delta)).astype(jnp.bfloat16)
        dkey = dot(ds, qs, (1, 0))
        t2[0, h] = dkey[:ROWS].astype(jnp.bfloat16)
        back[0, h, 0] = back_send(0, h, 0)
        back[0, h, 0].start()
        t1[0, h] = dkey[ROWS : 2 * ROWS]
        t0[0, h] = dkey[2 * ROWS :]
        ot = dot(vals, p16, (0, 0))
        qt = dot(keys, ds, (0, 0)) * SCALE
        for i in range(GROUP):
            at = slice(h * WIDE + i * D, h * WIDE + (i + 1) * D)
            o[:, at] = ot[:, i * D : (i + 1) * D].T.astype(jnp.bfloat16)
            dq[:, at] = qt[:, i * D : (i + 1) * D].T.astype(jnp.bfloat16)
        store(o.at[:, wide], o_hbm.at[:, wide], h * 2)
        store(dq.at[:, wide], dq_hbm.at[:, wide], h * 2 + 1)

    def middle(h):
        for i in (1, 0):
            back[0, h, i].wait_recv()
            u[i, h] = (t1[i, h] + r2[i, h].astype(jnp.float32)).astype(jnp.bfloat16)
            back[1, h, i] = back_send(1, h, i)
            back[1, h, i].start()

    def last(h):
        cols = pl.ds(h * D, D)
        for i in (1, 0):
            back[1, h, i].wait_recv()
            full = t0[i, h] + ru[i, h].astype(jnp.float32)
            if i == 0:
                full = full * SCALE
            dkv[i, :, cols] = full.astype(jnp.bfloat16)
            store(dkv.at[i, :, cols], (dk_hbm, dv_hbm)[i].at[:, cols], 8 + h * 2 + i)

    head(0)
    relay_on(2)
    relay_on(3)
    head(1)
    middle(0)
    head(2)
    middle(1)
    last(0)
    head(3)
    middle(2)
    last(1)
    middle(3)
    last(2)
    last(3)

    for h in range(KV_HEADS):
        for c in own[h] + relay[h]:
            c.wait_send()
        for stage in range(2):
            for i in range(2):
                back[stage, h, i].wait_send()
    for c in [m1] + m2 + m3:
        c.wait_send()
    for c in stores:
        c.wait()


def on_device(queries, keys, values, output_gradient, doc_blocks, doc_pad):
    hbm = pl.BlockSpec(memory_space=pltpu.HBM)
    bf16, f32 = jnp.bfloat16, jnp.float32
    terms = (2, KV_HEADS, ROWS, D)
    return pl.pallas_call(
        body,
        out_shape=(
            jax.ShapeDtypeStruct(queries.shape, bf16),
            jax.ShapeDtypeStruct(queries.shape, bf16),
            jax.ShapeDtypeStruct(keys.shape, bf16),
            jax.ShapeDtypeStruct(keys.shape, bf16),
        ),
        in_specs=[hbm] * 6,
        out_specs=(pl.BlockSpec(memory_space=pl.ANY),) * 4,
        scratch_shapes=[
            pltpu.VMEM(queries.shape, bf16),
            pltpu.VMEM(queries.shape, bf16),
            pltpu.VMEM((2, KV_HEADS, 3 * ROWS, D), bf16),
            pltpu.VMEM((1, 16), jnp.int32),
            pltpu.VMEM((1, 16), jnp.int32),
            pltpu.VMEM((DP, 2, 128), jnp.int32),
            pltpu.VMEM(terms, bf16),
            pltpu.VMEM(terms, bf16),
            pltpu.VMEM(terms, bf16),
            pltpu.VMEM(terms, bf16),
            pltpu.VMEM(terms, f32),
            pltpu.VMEM(terms, f32),
            pltpu.VMEM(queries.shape, bf16),
            pltpu.VMEM(queries.shape, bf16),
            pltpu.VMEM((2, ROWS, KV_HEADS * D), bf16),
            pltpu.SemaphoreType.DMA((18,)),
            pltpu.SemaphoreType.DMA((16,)),
            pltpu.SemaphoreType.DMA((2, KV_HEADS, 2)),
            pltpu.SemaphoreType.DMA((2, KV_HEADS, 2)),
            pltpu.SemaphoreType.DMA((2, KV_HEADS, 2)),
            pltpu.SemaphoreType.DMA((2, KV_HEADS, 2)),
            pltpu.SemaphoreType.DMA((X + Y - 1,)),
            pltpu.SemaphoreType.DMA((X + Y - 1,)),
        ],
        compiler_params=pltpu.CompilerParams(
            collective_id=0, has_side_effects=True, vmem_limit_bytes=40 * 1024 * 1024
        ),
    )(*[
        pltpu.with_memory_space_constraint(a, pltpu.HBM)
        for a in (
            queries, keys, values, output_gradient,
            doc_blocks.reshape(1, 16), doc_pad.reshape(1, 16),
        )
    ])


def solution(mesh):
    tokens = P(("dp", "ctx"), None)
    return jax.shard_map(
        on_device,
        mesh=mesh,
        in_specs=(tokens, tokens, tokens, tokens, P("dp"), P("dp")),
        out_specs=(tokens, tokens, tokens, tokens),
        check_vma=False,
    )
```

```python
import jax
import jax.numpy as jnp
from jax import lax
from jax.experimental import pallas as pl
from jax.experimental.pallas import tpu as pltpu
from jax.sharding import PartitionSpec as P

KV_HEADS = 4
GROUP = 4
D = 128
ROWS = 128
WIDE = GROUP * D
SCALE = D**-0.5
LOG2E = 1.4426950408889634
NEG = -1e30
X = 4
Y = 4
DP = 32
CTX = 32
MESH = pl.DeviceIdType.MESH


def dot(a, b, contract):
    return lax.dot_general(
        a, b, ((contract[:1], contract[1:]), ((), ())), preferred_element_type=jnp.float32
    )


def stacked(ref, h):
    return jnp.concatenate(
        [ref[:, h * WIDE + g * D : h * WIDE + (g + 1) * D] for g in range(GROUP)], axis=0
    )


def body(
    q_hbm, k_hbm, v_hbm, g_hbm, size_hbm, pad_hbm,
    o, dq, dk, dv,
    q, g, kv, size_row, pad_row, meta, ex, dpr, stat,
    t2, r2, u, ru, t1, t0,
    in_sem, f_send, f_recv, b_send, b_recv, m_send, m_recv,
):
    dp, ctx = lax.axis_index("dp"), lax.axis_index("ctx")
    block = dp * CTX + ctx
    after = lax.rem(block + 1, DP * CTX)
    ahead = (after // CTX, lax.rem(after, CTX))
    before = lax.rem(block + DP * CTX - 1, DP * CTX)
    behind = (before // CTX, lax.rem(before, CTX))
    core = lax.rem(dp, 2)
    x = lax.rem(dp // 2, X)
    y = dp // (2 * X)
    pair = (dp + 1 - 2 * core, ctx)
    along_x = [((y * X + lax.rem(x + j, X)) * 2 + core, ctx) for j in range(1, X)]
    along_y = [((lax.rem(y + j, Y) * X + x) * 2 + core, ctx) for j in range(1, Y)]

    barrier = pltpu.get_barrier_semaphore()
    peers = [pair] + along_x + along_y
    for peer in [behind] + peers:
        pl.semaphore_signal(barrier, inc=1, device_id=peer, device_id_type=MESH)

    tiny = [
        pltpu.make_async_copy(size_hbm, size_row, in_sem.at[0]),
        pltpu.make_async_copy(pad_hbm, pad_row, in_sem.at[1]),
    ]
    loads = []
    for h in range(KV_HEADS):
        cols = pl.ds(h * D, D)
        wide = pl.ds(h * WIDE, WIDE)
        loads.append([
            pltpu.make_async_copy(
                k_hbm.at[:, cols], kv.at[0, h, pl.ds(2 * ROWS, ROWS)], in_sem.at[4 + h * 4]),
            pltpu.make_async_copy(q_hbm.at[:, wide], q.at[:, wide], in_sem.at[2 + h * 4]),
            pltpu.make_async_copy(
                v_hbm.at[:, cols], kv.at[1, h, pl.ds(2 * ROWS, ROWS)], in_sem.at[5 + h * 4]),
            pltpu.make_async_copy(g_hbm.at[:, wide], g.at[:, wide], in_sem.at[3 + h * 4]),
        ])
    for group in [tiny] + loads:
        for c in group:
            c.start()
    meta[pl.ds(dp, 1)] = jnp.zeros((1, 2, 128), jnp.int32)
    for c in tiny:
        c.wait()
    meta[pl.ds(dp, 1), 0:1, 0:16] = size_row[...].reshape(1, 1, 16)
    meta[pl.ds(dp, 1), 1:2, 0:16] = pad_row[...].reshape(1, 1, 16)
    pl.semaphore_wait(barrier, 1 + len(peers))

    def own_send(h):
        return [
            pltpu.make_async_remote_copy(
                src_ref=(k_hbm, v_hbm)[i].at[:, pl.ds(h * D, D)],
                dst_ref=kv.at[i, h, pl.ds(ROWS, ROWS)],
                send_sem=f_send.at[0, h, i], recv_sem=f_recv.at[0, h, i],
                device_id=ahead, device_id_type=MESH)
            for i in range(2)
        ]

    def relay_send(h):
        return [
            pltpu.make_async_remote_copy(
                src_ref=kv.at[i, h, pl.ds(ROWS, ROWS)],
                dst_ref=kv.at[i, h, pl.ds(0, ROWS)],
                send_sem=f_send.at[1, h, i], recv_sem=f_recv.at[1, h, i],
                device_id=ahead, device_id_type=MESH)
            for i in range(2)
        ]

    def back_send(stage, h, i):
        return pltpu.make_async_remote_copy(
            src_ref=(t2, u)[stage].at[i, h], dst_ref=(r2, ru)[stage].at[i, h],
            send_sem=b_send.at[stage, h, i], recv_sem=b_recv.at[stage, h, i],
            device_id=behind, device_id_type=MESH)

    def meta_send(first, count, device, slot):
        rows = meta.at[pl.ds(first, count)]
        return pltpu.make_async_remote_copy(
            src_ref=rows, dst_ref=rows, send_sem=m_send.at[slot], recv_sem=m_recv.at[slot],
            device_id=device, device_id_type=MESH)

    own = [own_send(h) for h in range(KV_HEADS)]
    relay = [relay_send(h) for h in range(KV_HEADS)]

    def start(copies):
        for c in copies:
            c.start()

    def relay_on(h):
        for a, b in zip(own[h], relay[h]):
            a.wait_recv()
            b.start()

    stacks = {}

    def part(h, at):
        rows = slice((2 - at) * ROWS, (3 - at) * ROWS)
        qs, gs = stacked(q, h), stacked(g, h)
        s = dot(kv[0, h, rows], qs, (1, 1)) * (SCALE * LOG2E)
        if at == 0:
            s = s + jnp.concatenate([tri] * GROUP, axis=1)
        peak = jnp.max(s, axis=0, keepdims=True)
        e = jnp.exp2(s - peak)
        r = dot(kv[1, h, rows], gs, (1, 1))
        ex[h, rows] = e
        dpr[h, rows] = r
        stat[h, at, 0:1] = peak
        stat[h, at, 1:2] = jnp.sum(e, axis=0, keepdims=True)
        stat[h, at, 2:3] = jnp.sum(e * r, axis=0, keepdims=True)

    tri = jnp.where(
        lax.broadcasted_iota(jnp.int32, (ROWS, ROWS), 0)
        <= lax.broadcasted_iota(jnp.int32, (ROWS, ROWS), 1),
        0.0, NEG,
    )

    m1 = meta_send(dp, 1, pair, 0)
    m1.start()
    for h in range(KV_HEADS):
        start(own[h])
    for c in loads[0]:
        c.wait()
    part(0, 0)
    meta_send(dp + 1 - 2 * core, 1, pair, 0).wait_recv()
    m2 = [meta_send(dp - core, 2, along_x[j - 1], j) for j in range(1, X)]
    start(m2)
    for c in loads[1]:
        c.wait()
    part(1, 0)
    for j in range(1, X):
        meta_send((y * X + lax.rem(x + X - j, X)) * 2, 2, pair, j).wait_recv()
    m3 = [meta_send(y * X * 2, 2 * X, along_y[j - 1], X - 1 + j) for j in range(1, Y)]
    start(m3)
    relay_on(0)
    for c in loads[2]:
        c.wait()
    part(2, 0)
    relay_on(1)
    for c in loads[3]:
        c.wait()
    part(3, 0)
    relay_on(2)
    part(0, 1)
    for j in range(1, Y):
        meta_send(lax.rem(y + Y - j, Y) * X * 2, 2 * X, pair, X - 1 + j).wait_recv()
    relay_on(3)

    sizes = meta[:, 0, :].astype(jnp.float32)
    pads = meta[:, 1, :].astype(jnp.float32)
    sizes16 = sizes.astype(jnp.bfloat16)
    below = (
        lax.broadcasted_iota(jnp.int32, (128, 128), 0)
        < lax.broadcasted_iota(jnp.int32, (128, 128), 1)
    )
    inside = dot(sizes16, jnp.where(below, 1.0, 0.0).astype(jnp.bfloat16), (1, 0))
    totals = dot(sizes16, jnp.ones((128, 128), jnp.bfloat16), (1, 0))
    over = (
        lax.broadcasted_iota(jnp.int32, (DP, DP), 1)
        < lax.broadcasted_iota(jnp.int32, (DP, DP), 0)
    )
    lead = dot(
        jnp.where(over, 1.0, 0.0).astype(jnp.bfloat16), totals.astype(jnp.bfloat16), (1, 0)
    )
    offset = block.astype(jnp.float32) - (inside + lead)
    mine = (offset >= 0.0) & (offset < sizes)

    def total(a):
        return jnp.sum(jnp.sum(a, axis=0, keepdims=True), axis=1, keepdims=True)

    place = total(jnp.where(mine, offset, 0.0))
    valid = total(
        jnp.where(mine, jnp.minimum((sizes - offset) * float(ROWS) - pads, float(ROWS)), 0.0)
    )
    bias = [None, jnp.where(place >= 0.5, 0.0, NEG), jnp.where(place >= 1.5, 0.0, NEG)]
    slot = lax.broadcasted_iota(jnp.int32, (1, ROWS), 1).astype(jnp.float32)
    live1 = jnp.where(slot < valid, 1.0, 0.0)
    live = jnp.concatenate([live1] * GROUP, axis=1)

    back = {}

    def send_back(stage, h, i):
        back[stage, h, i] = back_send(stage, h, i)
        back[stage, h, i].start()

    def finish(h):
        qs, gs = stacked(q, h), stacked(g, h)
        peaks = [stat[h, 0, 0:1]] + [stat[h, at, 0:1] + bias[at] for at in (1, 2)]
        top = jnp.maximum(jnp.maximum(peaks[0], peaks[1]), peaks[2])
        w = [jnp.exp2(p - top) for p in peaks]
        whole = sum(w[at] * stat[h, at, 1:2] for at in range(3))
        share = live / whole
        delta = sum(w[at] * stat[h, at, 2:3] for at in range(3)) * share
        p16, ds16 = {}, {}
        for at in (2, 1, 0):
            rows = slice((2 - at) * ROWS, (3 - at) * ROWS)
            p = ex[h, rows] * (w[at] * share)
            p16[at] = p.astype(jnp.bfloat16)
            ds16[at] = (p * (dpr[h, rows] - delta)).astype(jnp.bfloat16)
            dval = dot(p16[at], gs, (1, 0))
            dkey = dot(ds16[at], qs, (1, 0))
            if at == 2:
                t2[1, h] = dval.astype(jnp.bfloat16)
                send_back(0, h, 1)
                t2[0, h] = dkey.astype(jnp.bfloat16)
                send_back(0, h, 0)
            else:
                keep = (t0, t1)[at]
                keep[1, h] = dval
                keep[0, h] = dkey
        stacks[h] = (
            jnp.concatenate([p16[2], p16[1], p16[0]], axis=0),
            jnp.concatenate([ds16[2], ds16[1], ds16[0]], axis=0),
        )

    def outputs(h):
        p16, ds16 = stacks[h]
        ot = dot(kv[1, h], p16, (0, 0))
        qt = dot(kv[0, h], ds16, (0, 0)) * SCALE
        for i in range(GROUP):
            at = slice(h * WIDE + i * D, h * WIDE + (i + 1) * D)
            o[:, at] = ot[:, i * D : (i + 1) * D].T.astype(jnp.bfloat16)
            dq[:, at] = qt[:, i * D : (i + 1) * D].T.astype(jnp.bfloat16)

    def head(h):
        for c in relay[h]:
            c.wait_recv()
        part(h, 2)
        finish(h)
        outputs(h)

    def middle(h):
        for i in (1, 0):
            back[0, h, i].wait_recv()
            u[i, h] = (t1[i, h] + r2[i, h].astype(jnp.float32)).astype(jnp.bfloat16)
            send_back(1, h, i)

    def last(h):
        cols = slice(h * D, (h + 1) * D)
        for i in (1, 0):
            back[1, h, i].wait_recv()
            full = t0[i, h] + ru[i, h].astype(jnp.float32)
            if i == 0:
                dk[:, cols] = (full * SCALE).astype(jnp.bfloat16)
            else:
                dv[:, cols] = full.astype(jnp.bfloat16)

    part(1, 1)
    part(2, 1)
    part(3, 1)
    head(0)
    head(1)
    middle(0)
    head(2)
    middle(1)
    last(0)
    head(3)
    middle(2)
    last(1)
    middle(3)
    last(2)
    last(3)

    for h in range(KV_HEADS):
        for c in own[h] + relay[h]:
            c.wait_send()
        for stage in range(2):
            for i in range(2):
                back[stage, h, i].wait_send()
    for c in [m1] + m2 + m3:
        c.wait_send()


def write_out(*refs):
    sources, targets, sem = refs[:4], refs[4:8], refs[8]
    copies = [
        pltpu.make_async_copy(a, b, sem.at[i])
        for i, (a, b) in enumerate(zip(sources, targets))
    ]
    for c in copies:
        c.start()
    for c in copies:
        c.wait()


def on_device(queries, keys, values, output_gradient, doc_blocks, doc_pad):
    hbm = pl.BlockSpec(memory_space=pltpu.HBM)
    anywhere = pl.BlockSpec(memory_space=pl.ANY)
    bf16, f32 = jnp.bfloat16, jnp.float32
    terms = (2, KV_HEADS, ROWS, D)
    scores = (KV_HEADS, 3 * ROWS, WIDE)
    shapes = (queries.shape, queries.shape, keys.shape, keys.shape)
    results = pl.pallas_call(
        body,
        out_shape=tuple(jax.ShapeDtypeStruct(shape, bf16) for shape in shapes),
        in_specs=[hbm] * 6,
        out_specs=(pl.BlockSpec(memory_space=pltpu.VMEM),) * 4,
        scratch_shapes=[
            pltpu.VMEM(queries.shape, bf16),
            pltpu.VMEM(queries.shape, bf16),
            pltpu.VMEM((2, KV_HEADS, 3 * ROWS, D), bf16),
            pltpu.VMEM((1, 16), jnp.int32),
            pltpu.VMEM((1, 16), jnp.int32),
            pltpu.VMEM((DP, 2, 128), jnp.int32),
            pltpu.VMEM(scores, f32),
            pltpu.VMEM(scores, f32),
            pltpu.VMEM((KV_HEADS, 3, 8, WIDE), f32),
            pltpu.VMEM(terms, bf16),
            pltpu.VMEM(terms, bf16),
            pltpu.VMEM(terms, bf16),
            pltpu.VMEM(terms, bf16),
            pltpu.VMEM(terms, f32),
            pltpu.VMEM(terms, f32),
            pltpu.SemaphoreType.DMA((18,)),
            pltpu.SemaphoreType.DMA((2, KV_HEADS, 2)),
            pltpu.SemaphoreType.DMA((2, KV_HEADS, 2)),
            pltpu.SemaphoreType.DMA((2, KV_HEADS, 2)),
            pltpu.SemaphoreType.DMA((2, KV_HEADS, 2)),
            pltpu.SemaphoreType.DMA((X + Y - 1,)),
            pltpu.SemaphoreType.DMA((X + Y - 1,)),
        ],
        compiler_params=pltpu.CompilerParams(
            collective_id=0, has_side_effects=True, vmem_limit_bytes=40 * 1024 * 1024
        ),
    )(*[
        pltpu.with_memory_space_constraint(a, pltpu.HBM)
        for a in (
            queries, keys, values, output_gradient,
            doc_blocks.reshape(1, 16), doc_pad.reshape(1, 16),
        )
    ])
    return pl.pallas_call(
        write_out,
        out_shape=tuple(jax.ShapeDtypeStruct(shape, bf16) for shape in shapes),
        in_specs=[pl.BlockSpec(memory_space=pltpu.VMEM)] * 4,
        out_specs=(anywhere,) * 4,
        scratch_shapes=[pltpu.SemaphoreType.DMA((4,))],
    )(*[pltpu.with_memory_space_constraint(a, pltpu.VMEM) for a in results])


def solution(mesh):
    tokens = P(("dp", "ctx"), None)
    return jax.shard_map(
        on_device,
        mesh=mesh,
        in_specs=(tokens, tokens, tokens, tokens, P("dp"), P("dp")),
        out_specs=(tokens, tokens, tokens, tokens),
        check_vma=False,
    )
```

```python
import jax
import jax.numpy as jnp
from jax import lax
from jax.experimental import pallas as pl
from jax.experimental.pallas import tpu as pltpu
from jax.sharding import PartitionSpec as P

KV_HEADS = 4
GROUP = 4
D = 128
ROWS = 128
WIDE = GROUP * D
SCALE = D**-0.5
LOG2E = 1.4426950408889634
NEG = -1e30
X = 4
Y = 4
DP = 32
CTX = 32
MESH = pl.DeviceIdType.MESH


def dot(a, b, contract):
    return lax.dot_general(
        a, b, ((contract[:1], contract[1:]), ((), ())), preferred_element_type=jnp.float32
    )


def stacked(ref, h):
    return jnp.concatenate(
        [ref[:, h * WIDE + g * D : h * WIDE + (g + 1) * D] for g in range(GROUP)], axis=0
    )


def body(
    q_hbm, k_hbm, v_hbm, g_hbm, size_hbm, pad_hbm,
    o, dq, dk, dv,
    q, g, kv, size_row, pad_row, meta, ex, dpr, stat,
    t2, r2, u, ru, t1, t0,
    in_sem, f_send, f_recv, b_send, b_recv, m_send, m_recv,
):
    dp, ctx = lax.axis_index("dp"), lax.axis_index("ctx")
    block = dp * CTX + ctx
    after = lax.rem(block + 1, DP * CTX)
    ahead = (after // CTX, lax.rem(after, CTX))
    before = lax.rem(block + DP * CTX - 1, DP * CTX)
    behind = (before // CTX, lax.rem(before, CTX))
    core = lax.rem(dp, 2)
    x = lax.rem(dp // 2, X)
    y = dp // (2 * X)
    pair = (dp + 1 - 2 * core, ctx)
    along_x = [((y * X + lax.rem(x + j, X)) * 2 + core, ctx) for j in range(1, X)]
    along_y = [((lax.rem(y + j, Y) * X + x) * 2 + core, ctx) for j in range(1, Y)]

    barrier = pltpu.get_barrier_semaphore()
    peers = [pair] + along_x + along_y
    in_plane = (ctx > 0) & (ctx < CTX - 2)
    told = jnp.logical_not(in_plane)
    pl.semaphore_signal(barrier, inc=1, device_id=behind, device_id_type=MESH)

    @pl.when(in_plane)
    def _():
        for peer in peers:
            pl.semaphore_signal(barrier, inc=1, device_id=peer, device_id_type=MESH)


    tiny = [
        pltpu.make_async_copy(size_hbm, size_row, in_sem.at[0]),
        pltpu.make_async_copy(pad_hbm, pad_row, in_sem.at[1]),
    ]
    loads = []
    for h in range(KV_HEADS):
        cols = pl.ds(h * D, D)
        wide = pl.ds(h * WIDE, WIDE)
        loads.append([
            pltpu.make_async_copy(
                k_hbm.at[:, cols], kv.at[0, h, pl.ds(2 * ROWS, ROWS)], in_sem.at[4 + h * 4]),
            pltpu.make_async_copy(q_hbm.at[:, wide], q.at[:, wide], in_sem.at[2 + h * 4]),
            pltpu.make_async_copy(
                v_hbm.at[:, cols], kv.at[1, h, pl.ds(2 * ROWS, ROWS)], in_sem.at[5 + h * 4]),
            pltpu.make_async_copy(g_hbm.at[:, wide], g.at[:, wide], in_sem.at[3 + h * 4]),
        ])
    for group in loads:
        group[0].start()
        group[2].start()
    for c in tiny:
        c.start()
    for group in loads:
        group[1].start()
        group[3].start()
    for c in tiny:
        c.wait()

    @pl.when(in_plane)
    def _():
        meta[pl.ds(dp, 1)] = jnp.zeros((1, 2, 128), jnp.int32)
        meta[pl.ds(dp, 1), 0:1, 0:16] = size_row[...].reshape(1, 1, 16)
        meta[pl.ds(dp, 1), 1:2, 0:16] = pad_row[...].reshape(1, 1, 16)

    for group in loads:
        group[0].wait()
        group[2].wait()

    @pl.when(told)
    def _():
        pl.semaphore_wait(barrier, 1)

    @pl.when(in_plane)
    def _():
        pl.semaphore_wait(barrier, 1 + len(peers))

    def own_send(h):
        return [
            pltpu.make_async_remote_copy(
                src_ref=kv.at[i, h, pl.ds(2 * ROWS, ROWS)],
                dst_ref=kv.at[i, h, pl.ds(ROWS, ROWS)],
                send_sem=f_send.at[0, h, i], recv_sem=f_recv.at[0, h, i],
                device_id=ahead, device_id_type=MESH)
            for i in range(2)
        ]

    def relay_send(h):
        return [
            pltpu.make_async_remote_copy(
                src_ref=kv.at[i, h, pl.ds(ROWS, ROWS)],
                dst_ref=kv.at[i, h, pl.ds(0, ROWS)],
                send_sem=f_send.at[1, h, i], recv_sem=f_recv.at[1, h, i],
                device_id=ahead, device_id_type=MESH)
            for i in range(2)
        ]

    def back_send(stage, h, i):
        return pltpu.make_async_remote_copy(
            src_ref=(t2, u)[stage].at[i, h], dst_ref=(r2, ru)[stage].at[i, h],
            send_sem=b_send.at[stage, h, i], recv_sem=b_recv.at[stage, h, i],
            device_id=behind, device_id_type=MESH)

    def meta_send(first, count, device, slot):
        rows = meta.at[pl.ds(first, count)]
        return pltpu.make_async_remote_copy(
            src_ref=rows, dst_ref=rows, send_sem=m_send.at[slot], recv_sem=m_recv.at[slot],
            device_id=device, device_id_type=MESH)

    own = [own_send(h) for h in range(KV_HEADS)]
    relay = [relay_send(h) for h in range(KV_HEADS)]

    def start(copies):
        for c in copies:
            c.start()

    def relay_on(h):
        for a, b in zip(own[h], relay[h]):
            a.wait_recv()
            b.start()

    stacks = {}

    def part(h, at):
        rows = slice((2 - at) * ROWS, (3 - at) * ROWS)
        qs, gs = stacked(q, h), stacked(g, h)
        s = dot(kv[0, h, rows], qs, (1, 1)) * (SCALE * LOG2E)
        if at == 0:
            s = s + jnp.concatenate([tri] * GROUP, axis=1)
        peak = jnp.max(s, axis=0, keepdims=True)
        e = jnp.exp2(s - peak)
        r = dot(kv[1, h, rows], gs, (1, 1))
        ex[h, rows] = e
        dpr[h, rows] = r
        stat[h, at, 0:1] = peak
        stat[h, at, 1:2] = jnp.sum(e, axis=0, keepdims=True)
        stat[h, at, 2:3] = jnp.sum(e * r, axis=0, keepdims=True)

    tri = jnp.where(
        lax.broadcasted_iota(jnp.int32, (ROWS, ROWS), 0)
        <= lax.broadcasted_iota(jnp.int32, (ROWS, ROWS), 1),
        0.0, NEG,
    )

    m1 = meta_send(dp, 1, pair, 0)
    m2 = [meta_send(dp - core, 2, along_x[j - 1], j) for j in range(1, X)]
    m3 = [meta_send(y * X * 2, 2 * X, along_y[j - 1], X - 1 + j) for j in range(1, Y)]
    table = pltpu.make_async_remote_copy(
        src_ref=meta, dst_ref=meta, send_sem=m_send.at[X + Y - 1], recv_sem=m_recv.at[X + Y - 1],
        device_id=behind, device_id_type=MESH)

    def exchange_x():
        @pl.when(in_plane)
        def _():
            meta_send(dp + 1 - 2 * core, 1, pair, 0).wait_recv()
            start(m2)

    def exchange_y():
        @pl.when(in_plane)
        def _():
            for j in range(1, X):
                meta_send((y * X + lax.rem(x + X - j, X)) * 2, 2, pair, j).wait_recv()
            start(m3)

    def exchanged():
        @pl.when(in_plane)
        def _():
            for j in range(1, Y):
                meta_send(lax.rem(y + Y - j, Y) * X * 2, 2 * X, pair, X - 1 + j).wait_recv()

    def wait_rest(h):
        loads[h][1].wait()
        loads[h][3].wait()

    pl.when(in_plane)(m1.start)
    def sent(h):
        for c in own[h]:
            c.wait_send()

    start(own[0])
    start(own[1])
    wait_rest(0)
    part(0, 0)
    sent(0)
    start(own[2])
    exchange_x()
    wait_rest(1)
    part(1, 0)
    exchange_y()
    wait_rest(2)
    part(2, 0)
    sent(1)
    wait_rest(3)
    part(3, 0)
    start(own[3])
    relay_on(0)

    @pl.when(ctx == 0)
    def _():
        table.wait_recv()
        table.start()

    relay_on(1)
    part(0, 1)
    relay_on(2)
    part(1, 1)
    exchanged()
    relay_on(3)
    pl.when(ctx == 1)(table.start)
    part(2, 1)
    part(3, 1)
    pl.when(ctx >= CTX - 2)(table.wait_recv)
    pl.when(ctx == CTX - 1)(table.start)

    sizes = meta[:, 0, :].astype(jnp.float32)
    pads = meta[:, 1, :].astype(jnp.float32)
    sizes16 = sizes.astype(jnp.bfloat16)
    below = (
        lax.broadcasted_iota(jnp.int32, (128, 128), 0)
        < lax.broadcasted_iota(jnp.int32, (128, 128), 1)
    )
    inside = dot(sizes16, jnp.where(below, 1.0, 0.0).astype(jnp.bfloat16), (1, 0))
    totals = dot(sizes16, jnp.ones((128, 128), jnp.bfloat16), (1, 0))
    over = (
        lax.broadcasted_iota(jnp.int32, (DP, DP), 1)
        < lax.broadcasted_iota(jnp.int32, (DP, DP), 0)
    )
    lead = dot(
        jnp.where(over, 1.0, 0.0).astype(jnp.bfloat16), totals.astype(jnp.bfloat16), (1, 0)
    )
    offset = block.astype(jnp.float32) - (inside + lead)
    mine = (offset >= 0.0) & (offset < sizes)

    def total(a):
        return jnp.sum(jnp.sum(a, axis=0, keepdims=True), axis=1, keepdims=True)

    place = total(jnp.where(mine, offset, 0.0))
    valid = total(
        jnp.where(mine, jnp.minimum((sizes - offset) * float(ROWS) - pads, float(ROWS)), 0.0)
    )
    bias = [None, jnp.where(place >= 0.5, 0.0, NEG), jnp.where(place >= 1.5, 0.0, NEG)]
    slot = lax.broadcasted_iota(jnp.int32, (1, ROWS), 1).astype(jnp.float32)
    live1 = jnp.where(slot < valid, 1.0, 0.0)
    live = jnp.concatenate([live1] * GROUP, axis=1)

    def send_back(stage, h, i):
        back_send(stage, h, i).start()

    def finish(h):
        qs, gs = stacked(q, h), stacked(g, h)
        peaks = [stat[h, 0, 0:1]] + [stat[h, at, 0:1] + bias[at] for at in (1, 2)]
        top = jnp.maximum(jnp.maximum(peaks[0], peaks[1]), peaks[2])
        w = [jnp.exp2(p - top) for p in peaks]
        whole = sum(w[at] * stat[h, at, 1:2] for at in range(3))
        share = live / whole
        delta = sum(w[at] * stat[h, at, 2:3] for at in range(3)) * share
        p16, ds16 = {}, {}
        for at in (2, 1, 0):
            rows = slice((2 - at) * ROWS, (3 - at) * ROWS)
            p = ex[h, rows] * (w[at] * share)
            p16[at] = p.astype(jnp.bfloat16)
            ds16[at] = (p * (dpr[h, rows] - delta)).astype(jnp.bfloat16)
            dval = dot(p16[at], gs, (1, 0))
            dkey = dot(ds16[at], qs, (1, 0))
            if at == 2:
                t2[1, h] = dval.astype(jnp.bfloat16)
                send_back(0, h, 1)
                t2[0, h] = dkey.astype(jnp.bfloat16)
                send_back(0, h, 0)
            else:
                keep = (t0, t1)[at]
                keep[1, h] = dval
                keep[0, h] = dkey
        stacks[h] = (
            jnp.concatenate([p16[2], p16[1], p16[0]], axis=0),
            jnp.concatenate([ds16[2], ds16[1], ds16[0]], axis=0),
        )

    def outputs(h):
        p16, ds16 = stacks[h]
        ot = dot(kv[1, h], p16, (0, 0))
        qt = dot(kv[0, h], ds16, (0, 0)) * SCALE
        for i in range(GROUP):
            at = slice(h * WIDE + i * D, h * WIDE + (i + 1) * D)
            o[:, at] = ot[:, i * D : (i + 1) * D].T.astype(jnp.bfloat16)
            dq[:, at] = qt[:, i * D : (i + 1) * D].T.astype(jnp.bfloat16)

    def head(h):
        for c in relay[h]:
            c.wait_recv()
        part(h, 2)
        finish(h)
        outputs(h)

    def middle(h):
        for i in (1, 0):
            back_send(0, h, i).wait_recv()
            u[i, h] = (t1[i, h] + r2[i, h].astype(jnp.float32)).astype(jnp.bfloat16)
            send_back(1, h, i)

    def last(h):
        cols = slice(h * D, (h + 1) * D)
        for i in (1, 0):
            back_send(1, h, i).wait_recv()
            full = t0[i, h] + ru[i, h].astype(jnp.float32)
            if i == 0:
                dk[:, cols] = (full * SCALE).astype(jnp.bfloat16)
            else:
                dv[:, cols] = full.astype(jnp.bfloat16)

    second = ctx == 1

    def middle_if(h, when):
        pl.when(when)(lambda: middle(h))

    first = ctx == 0
    usual = ctx > 1
    for h in range(KV_HEADS):
        head(h)
        middle_if(h, second)
        if h >= 1:
            middle_if(h - 1, first)
        if h == 2:
            middle_if(0, usual)
    middle_if(1, usual)
    middle_if(2, usual)
    middle_if(3, jnp.logical_not(second))
    for h in range(KV_HEADS):
        last(h)

    for h in range(KV_HEADS):
        for c in (own[h] if h > 1 else []) + relay[h]:
            c.wait_send()
        for stage in range(2):
            for i in range(2):
                back_send(stage, h, i).wait_send()

    @pl.when(in_plane)
    def _():
        for c in [m1] + m2 + m3:
            c.wait_send()

    pl.when((ctx <= 1) | (ctx == CTX - 1))(table.wait_send)


def write_out(*refs):
    sources, targets, sem = refs[:4], refs[4:8], refs[8]
    copies = [
        pltpu.make_async_copy(a, b, sem.at[i])
        for i, (a, b) in enumerate(zip(sources, targets))
    ]
    for c in copies:
        c.start()
    for c in copies:
        c.wait()


def on_device(queries, keys, values, output_gradient, doc_blocks, doc_pad):
    hbm = pl.BlockSpec(memory_space=pltpu.HBM)
    anywhere = pl.BlockSpec(memory_space=pl.ANY)
    bf16, f32 = jnp.bfloat16, jnp.float32
    terms = (2, KV_HEADS, ROWS, D)
    scores = (KV_HEADS, 3 * ROWS, WIDE)
    shapes = (queries.shape, queries.shape, keys.shape, keys.shape)
    results = pl.pallas_call(
        body,
        out_shape=tuple(jax.ShapeDtypeStruct(shape, bf16) for shape in shapes),
        in_specs=[hbm] * 6,
        out_specs=(pl.BlockSpec(memory_space=pltpu.VMEM),) * 4,
        scratch_shapes=[
            pltpu.VMEM(queries.shape, bf16),
            pltpu.VMEM(queries.shape, bf16),
            pltpu.VMEM((2, KV_HEADS, 3 * ROWS, D), bf16),
            pltpu.VMEM((1, 16), jnp.int32),
            pltpu.VMEM((1, 16), jnp.int32),
            pltpu.VMEM((DP, 2, 128), jnp.int32),
            pltpu.VMEM(scores, f32),
            pltpu.VMEM(scores, f32),
            pltpu.VMEM((KV_HEADS, 3, 8, WIDE), f32),
            pltpu.VMEM(terms, bf16),
            pltpu.VMEM(terms, bf16),
            pltpu.VMEM(terms, bf16),
            pltpu.VMEM(terms, bf16),
            pltpu.VMEM(terms, f32),
            pltpu.VMEM(terms, f32),
            pltpu.SemaphoreType.DMA((18,)),
            pltpu.SemaphoreType.DMA((2, KV_HEADS, 2)),
            pltpu.SemaphoreType.DMA((2, KV_HEADS, 2)),
            pltpu.SemaphoreType.DMA((2, KV_HEADS, 2)),
            pltpu.SemaphoreType.DMA((2, KV_HEADS, 2)),
            pltpu.SemaphoreType.DMA((X + Y,)),
            pltpu.SemaphoreType.DMA((X + Y,)),
        ],
        compiler_params=pltpu.CompilerParams(
            collective_id=0, has_side_effects=True, vmem_limit_bytes=40 * 1024 * 1024
        ),
    )(*[
        pltpu.with_memory_space_constraint(a, pltpu.HBM)
        for a in (
            queries, keys, values, output_gradient,
            doc_blocks.reshape(1, 16), doc_pad.reshape(1, 16),
        )
    ])
    return pl.pallas_call(
        write_out,
        out_shape=tuple(jax.ShapeDtypeStruct(shape, bf16) for shape in shapes),
        in_specs=[pl.BlockSpec(memory_space=pltpu.VMEM)] * 4,
        out_specs=(anywhere,) * 4,
        scratch_shapes=[pltpu.SemaphoreType.DMA((4,))],
    )(*[pltpu.with_memory_space_constraint(a, pltpu.VMEM) for a in results])


def solution(mesh):
    tokens = P(("dp", "ctx"), None)
    return jax.shard_map(
        on_device,
        mesh=mesh,
        in_specs=(tokens, tokens, tokens, tokens, P("dp"), P("dp")),
        out_specs=(tokens, tokens, tokens, tokens),
        check_vma=False,
    )
```

```python
import jax
import jax.numpy as jnp
from jax import lax
from jax.experimental import pallas as pl
from jax.experimental.pallas import tpu as pltpu
from jax.sharding import PartitionSpec as P

KV_HEADS = 4
GROUP = 4
D = 128
ROWS = 128
WIDE = GROUP * D
SCALE = D**-0.5
LOG2E = 1.4426950408889634
NEG = -1e30
X = 4
Y = 4
DP = 32
CTX = 32
MESH = pl.DeviceIdType.MESH


def dot(a, b, contract):
    return lax.dot_general(
        a, b, ((contract[:1], contract[1:]), ((), ())), preferred_element_type=jnp.float32
    )


def stacked(ref, h):
    return jnp.concatenate(
        [ref[:, h * WIDE + g * D : h * WIDE + (g + 1) * D] for g in range(GROUP)], axis=0
    )


def body(
    q_hbm, k_hbm, v_hbm, g_hbm, size_hbm, pad_hbm,
    o, dq, dk, dv,
    q, g, kv, size_row, pad_row, meta, ex, dpr, stat, probs, dscores,
    t2, r2, u, ru, t1, t0,
    in_sem, f_send, f_recv, b_send, b_recv, m_send, m_recv,
):
    dp, ctx = lax.axis_index("dp"), lax.axis_index("ctx")
    block = dp * CTX + ctx
    after = lax.rem(block + 1, DP * CTX)
    ahead = (after // CTX, lax.rem(after, CTX))
    before = lax.rem(block + DP * CTX - 1, DP * CTX)
    behind = (before // CTX, lax.rem(before, CTX))
    core = lax.rem(dp, 2)
    x = lax.rem(dp // 2, X)
    y = dp // (2 * X)
    pair = (dp + 1 - 2 * core, ctx)
    along_x = [((y * X + lax.rem(x + j, X)) * 2 + core, ctx) for j in range(1, X)]
    along_y = [((lax.rem(y + j, Y) * X + x) * 2 + core, ctx) for j in range(1, Y)]

    barrier = pltpu.get_barrier_semaphore()
    peers = [pair] + along_x + along_y
    in_plane = (ctx > 0) & (ctx < CTX - 2)
    told = jnp.logical_not(in_plane)
    pl.semaphore_signal(barrier, inc=1, device_id=behind, device_id_type=MESH)

    @pl.when(in_plane)
    def _():
        for peer in peers:
            pl.semaphore_signal(barrier, inc=1, device_id=peer, device_id_type=MESH)


    tiny = [
        pltpu.make_async_copy(size_hbm, size_row, in_sem.at[0]),
        pltpu.make_async_copy(pad_hbm, pad_row, in_sem.at[1]),
    ]
    loads = []
    for h in range(KV_HEADS):
        cols = pl.ds(h * D, D)
        wide = pl.ds(h * WIDE, WIDE)
        loads.append([
            pltpu.make_async_copy(
                k_hbm.at[:, cols], kv.at[0, h, pl.ds(2 * ROWS, ROWS)], in_sem.at[4 + h * 4]),
            pltpu.make_async_copy(q_hbm.at[:, wide], q.at[:, wide], in_sem.at[2 + h * 4]),
            pltpu.make_async_copy(
                v_hbm.at[:, cols], kv.at[1, h, pl.ds(2 * ROWS, ROWS)], in_sem.at[5 + h * 4]),
            pltpu.make_async_copy(g_hbm.at[:, wide], g.at[:, wide], in_sem.at[3 + h * 4]),
        ])
    for group in loads:
        group[0].start()
        group[2].start()
    for c in tiny:
        c.start()
    for group in loads:
        group[1].start()
        group[3].start()
    for c in tiny:
        c.wait()

    @pl.when(in_plane)
    def _():
        meta[pl.ds(dp, 1)] = jnp.zeros((1, 2, 128), jnp.int32)
        meta[pl.ds(dp, 1), 0:1, 0:16] = size_row[...].reshape(1, 1, 16)
        meta[pl.ds(dp, 1), 1:2, 0:16] = pad_row[...].reshape(1, 1, 16)

    @pl.when(told)
    def _():
        pl.semaphore_wait(barrier, 1)

    @pl.when(in_plane)
    def _():
        pl.semaphore_wait(barrier, 1 + len(peers))

    def own_send(h):
        return [
            pltpu.make_async_remote_copy(
                src_ref=kv.at[i, h, pl.ds(2 * ROWS, ROWS)],
                dst_ref=kv.at[i, h, pl.ds(ROWS, ROWS)],
                send_sem=f_send.at[0, h, i], recv_sem=f_recv.at[0, h, i],
                device_id=ahead, device_id_type=MESH)
            for i in range(2)
        ]

    def relay_send(h):
        return [
            pltpu.make_async_remote_copy(
                src_ref=kv.at[i, h, pl.ds(ROWS, ROWS)],
                dst_ref=kv.at[i, h, pl.ds(0, ROWS)],
                send_sem=f_send.at[1, h, i], recv_sem=f_recv.at[1, h, i],
                device_id=ahead, device_id_type=MESH)
            for i in range(2)
        ]

    def back_send(stage, h, i):
        return pltpu.make_async_remote_copy(
            src_ref=(t2, u)[stage].at[i, h], dst_ref=(r2, ru)[stage].at[i, h],
            send_sem=b_send.at[stage, h, i], recv_sem=b_recv.at[stage, h, i],
            device_id=behind, device_id_type=MESH)

    def meta_send(first, count, device, slot):
        rows = meta.at[pl.ds(first, count)]
        return pltpu.make_async_remote_copy(
            src_ref=rows, dst_ref=rows, send_sem=m_send.at[slot], recv_sem=m_recv.at[slot],
            device_id=device, device_id_type=MESH)

    own = [own_send(h) for h in range(KV_HEADS)]
    relay = [relay_send(h) for h in range(KV_HEADS)]

    def start(copies):
        for c in copies:
            c.start()

    def relay_on(h):
        for a, b in zip(own[h], relay[h]):
            a.wait_recv()
            b.start()

    def part(h, at):
        rows = slice((2 - at) * ROWS, (3 - at) * ROWS)
        qs, gs = stacked(q, h), stacked(g, h)
        s = dot(kv[0, h, rows], qs, (1, 1)) * (SCALE * LOG2E)
        if at == 0:
            s = s + jnp.concatenate([tri] * GROUP, axis=1)
        peak = jnp.max(s, axis=0, keepdims=True)
        e = jnp.exp2(s - peak)
        r = dot(kv[1, h, rows], gs, (1, 1))
        ex[h, rows] = e
        dpr[h, rows] = r
        stat[h, at, 0:1] = peak
        stat[h, at, 1:2] = jnp.sum(e, axis=0, keepdims=True)
        stat[h, at, 2:3] = jnp.sum(e * r, axis=0, keepdims=True)

    tri = jnp.where(
        lax.broadcasted_iota(jnp.int32, (ROWS, ROWS), 0)
        <= lax.broadcasted_iota(jnp.int32, (ROWS, ROWS), 1),
        0.0, NEG,
    )

    m1 = meta_send(dp, 1, pair, 0)
    m2 = [meta_send(dp - core, 2, along_x[j - 1], j) for j in range(1, X)]
    m3 = [meta_send(y * X * 2, 2 * X, along_y[j - 1], X - 1 + j) for j in range(1, Y)]
    table = pltpu.make_async_remote_copy(
        src_ref=meta, dst_ref=meta, send_sem=m_send.at[X + Y - 1], recv_sem=m_recv.at[X + Y - 1],
        device_id=behind, device_id_type=MESH)

    def exchange_x():
        @pl.when(in_plane)
        def _():
            meta_send(dp + 1 - 2 * core, 1, pair, 0).wait_recv()
            start(m2)

    def exchange_y():
        @pl.when(in_plane)
        def _():
            for j in range(1, X):
                meta_send((y * X + lax.rem(x + X - j, X)) * 2, 2, pair, j).wait_recv()
            start(m3)

    def exchanged():
        @pl.when(in_plane)
        def _():
            for j in range(1, Y):
                meta_send(lax.rem(y + Y - j, Y) * X * 2, 2 * X, pair, X - 1 + j).wait_recv()

    def wait_rest(h):
        loads[h][1].wait()
        loads[h][3].wait()

    pl.when(in_plane)(m1.start)
    def sent(h):
        for c in own[h]:
            c.wait_send()

    def send_own(h):
        loads[h][0].wait()
        loads[h][2].wait()
        start(own[h])

    send_own(0)
    wait_rest(0)
    part(0, 0)
    sent(0)
    send_own(1)
    wait_rest(1)
    part(1, 0)
    sent(1)
    send_own(2)
    wait_rest(2)
    part(2, 0)
    exchange_x()
    sent(2)
    loads[3][0].wait()
    loads[3][2].wait()
    pl.when(ctx < CTX - 2)(lambda: start(own[3]))
    wait_rest(3)
    part(3, 0)
    exchange_y()
    relay_on(0)

    @pl.when(ctx == 0)
    def _():
        table.wait_recv()
        table.start()

    pl.when(ctx >= CTX - 2)(lambda: start(own[3]))
    relay_on(1)
    part(0, 1)
    relay_on(2)
    part(1, 1)
    exchanged()
    relay_on(3)
    pl.when(ctx == 1)(table.start)
    part(2, 1)
    part(3, 1)
    pl.when(ctx >= CTX - 2)(table.wait_recv)
    pl.when(ctx == CTX - 1)(table.start)

    sizes = meta[:, 0, :].astype(jnp.float32)
    pads = meta[:, 1, :].astype(jnp.float32)
    sizes16 = sizes.astype(jnp.bfloat16)
    below = (
        lax.broadcasted_iota(jnp.int32, (128, 128), 0)
        < lax.broadcasted_iota(jnp.int32, (128, 128), 1)
    )
    inside = dot(sizes16, jnp.where(below, 1.0, 0.0).astype(jnp.bfloat16), (1, 0))
    totals = dot(sizes16, jnp.ones((128, 128), jnp.bfloat16), (1, 0))
    over = (
        lax.broadcasted_iota(jnp.int32, (DP, DP), 1)
        < lax.broadcasted_iota(jnp.int32, (DP, DP), 0)
    )
    lead = dot(
        jnp.where(over, 1.0, 0.0).astype(jnp.bfloat16), totals.astype(jnp.bfloat16), (1, 0)
    )
    offset = block.astype(jnp.float32) - (inside + lead)
    mine = (offset >= 0.0) & (offset < sizes)

    def total(a):
        return jnp.sum(jnp.sum(a, axis=0, keepdims=True), axis=1, keepdims=True)

    place = total(jnp.where(mine, offset, 0.0))
    valid = total(
        jnp.where(mine, jnp.minimum((sizes - offset) * float(ROWS) - pads, float(ROWS)), 0.0)
    )
    bias = [None, jnp.where(place >= 0.5, 0.0, NEG), jnp.where(place >= 1.5, 0.0, NEG)]
    slot = lax.broadcasted_iota(jnp.int32, (1, ROWS), 1).astype(jnp.float32)
    live1 = jnp.where(slot < valid, 1.0, 0.0)
    live = jnp.concatenate([live1] * GROUP, axis=1)

    def send_back(stage, h, i):
        back_send(stage, h, i).start()

    def finish(h):
        qs, gs = stacked(q, h), stacked(g, h)
        peaks = [stat[h, 0, 0:1]] + [stat[h, at, 0:1] + bias[at] for at in (1, 2)]
        top = jnp.maximum(jnp.maximum(peaks[0], peaks[1]), peaks[2])
        w = [jnp.exp2(p - top) for p in peaks]
        whole = sum(w[at] * stat[h, at, 1:2] for at in range(3))
        share = live / whole
        delta = sum(w[at] * stat[h, at, 2:3] for at in range(3)) * share
        for at in (2, 1, 0):
            rows = slice((2 - at) * ROWS, (3 - at) * ROWS)
            p = ex[h, rows] * (w[at] * share)
            p16 = p.astype(jnp.bfloat16)
            ds16 = (p * (dpr[h, rows] - delta)).astype(jnp.bfloat16)
            probs[h, rows] = p16
            dscores[h, rows] = ds16
            dval = dot(p16, gs, (1, 0))
            dkey = dot(ds16, qs, (1, 0))
            if at == 2:
                t2[1, h] = dval.astype(jnp.bfloat16)
                send_back(0, h, 1)
                t2[0, h] = dkey.astype(jnp.bfloat16)
                send_back(0, h, 0)
            else:
                keep = (t0, t1)[at]
                keep[1, h] = dval
                keep[0, h] = dkey

    def outputs(h):
        ot = dot(kv[1, h], probs[h], (0, 0))
        qt = dot(kv[0, h], dscores[h], (0, 0)) * SCALE
        for i in range(GROUP):
            at = slice(h * WIDE + i * D, h * WIDE + (i + 1) * D)
            o[:, at] = ot[:, i * D : (i + 1) * D].T.astype(jnp.bfloat16)
            dq[:, at] = qt[:, i * D : (i + 1) * D].T.astype(jnp.bfloat16)

    def head(h):
        for c in relay[h]:
            c.wait_recv()
        part(h, 2)
        finish(h)

    def middle(h):
        for i in (1, 0):
            back_send(0, h, i).wait_recv()
            u[i, h] = (t1[i, h] + r2[i, h].astype(jnp.float32)).astype(jnp.bfloat16)
            send_back(1, h, i)

    def last(h):
        cols = slice(h * D, (h + 1) * D)
        for i in (1, 0):
            back_send(1, h, i).wait_recv()
            full = t0[i, h] + ru[i, h].astype(jnp.float32)
            if i == 0:
                dk[:, cols] = (full * SCALE).astype(jnp.bfloat16)
            else:
                dv[:, cols] = full.astype(jnp.bfloat16)

    second = ctx == 1

    def middle_if(h, when):
        pl.when(when)(lambda: middle(h))

    first = ctx == 0
    usual = ctx > 1
    for h in range(KV_HEADS):
        head(h)
        middle_if(h, second)
        if h >= 1:
            middle_if(h - 1, first)
        if h == 2:
            middle_if(0, usual)
    middle_if(1, usual)
    middle_if(2, usual)
    outputs(0)
    outputs(1)
    middle_if(3, jnp.logical_not(second))
    outputs(2)
    outputs(3)
    for h in range(KV_HEADS):
        last(h)

    for h in range(KV_HEADS):
        for c in (own[h] if h == KV_HEADS - 1 else []) + relay[h]:
            c.wait_send()
        for stage in range(2):
            for i in range(2):
                back_send(stage, h, i).wait_send()

    @pl.when(in_plane)
    def _():
        for c in [m1] + m2 + m3:
            c.wait_send()

    pl.when((ctx <= 1) | (ctx == CTX - 1))(table.wait_send)


def write_out(*refs):
    sources, targets, sem = refs[:4], refs[4:8], refs[8]
    copies = [
        pltpu.make_async_copy(a, b, sem.at[i])
        for i, (a, b) in enumerate(zip(sources, targets))
    ]
    for c in copies:
        c.start()
    for c in copies:
        c.wait()


def on_device(queries, keys, values, output_gradient, doc_blocks, doc_pad):
    hbm = pl.BlockSpec(memory_space=pltpu.HBM)
    anywhere = pl.BlockSpec(memory_space=pl.ANY)
    bf16, f32 = jnp.bfloat16, jnp.float32
    terms = (2, KV_HEADS, ROWS, D)
    scores = (KV_HEADS, 3 * ROWS, WIDE)
    shapes = (queries.shape, queries.shape, keys.shape, keys.shape)
    results = pl.pallas_call(
        body,
        out_shape=tuple(jax.ShapeDtypeStruct(shape, bf16) for shape in shapes),
        in_specs=[hbm] * 6,
        out_specs=(pl.BlockSpec(memory_space=pltpu.VMEM),) * 4,
        scratch_shapes=[
            pltpu.VMEM(queries.shape, bf16),
            pltpu.VMEM(queries.shape, bf16),
            pltpu.VMEM((2, KV_HEADS, 3 * ROWS, D), bf16),
            pltpu.VMEM((1, 16), jnp.int32),
            pltpu.VMEM((1, 16), jnp.int32),
            pltpu.VMEM((DP, 2, 128), jnp.int32),
            pltpu.VMEM(scores, f32),
            pltpu.VMEM(scores, f32),
            pltpu.VMEM((KV_HEADS, 3, 8, WIDE), f32),
            pltpu.VMEM(scores, bf16),
            pltpu.VMEM(scores, bf16),
            pltpu.VMEM(terms, bf16),
            pltpu.VMEM(terms, bf16),
            pltpu.VMEM(terms, bf16),
            pltpu.VMEM(terms, bf16),
            pltpu.VMEM(terms, f32),
            pltpu.VMEM(terms, f32),
            pltpu.SemaphoreType.DMA((18,)),
            pltpu.SemaphoreType.DMA((2, KV_HEADS, 2)),
            pltpu.SemaphoreType.DMA((2, KV_HEADS, 2)),
            pltpu.SemaphoreType.DMA((2, KV_HEADS, 2)),
            pltpu.SemaphoreType.DMA((2, KV_HEADS, 2)),
            pltpu.SemaphoreType.DMA((X + Y,)),
            pltpu.SemaphoreType.DMA((X + Y,)),
        ],
        compiler_params=pltpu.CompilerParams(
            collective_id=0, has_side_effects=True, vmem_limit_bytes=40 * 1024 * 1024
        ),
    )(*[
        pltpu.with_memory_space_constraint(a, pltpu.HBM)
        for a in (
            queries, keys, values, output_gradient,
            doc_blocks.reshape(1, 16), doc_pad.reshape(1, 16),
        )
    ])
    return pl.pallas_call(
        write_out,
        out_shape=tuple(jax.ShapeDtypeStruct(shape, bf16) for shape in shapes),
        in_specs=[pl.BlockSpec(memory_space=pltpu.VMEM)] * 4,
        out_specs=(anywhere,) * 4,
        scratch_shapes=[pltpu.SemaphoreType.DMA((4,))],
    )(*[pltpu.with_memory_space_constraint(a, pltpu.VMEM) for a in results])


def solution(mesh):
    tokens = P(("dp", "ctx"), None)
    return jax.shard_map(
        on_device,
        mesh=mesh,
        in_specs=(tokens, tokens, tokens, tokens, P("dp"), P("dp")),
        out_specs=(tokens, tokens, tokens, tokens),
        check_vma=False,
    )
```
